256 devices in a mesh: row: 8 (over z_hi, y), col: 4 (over z_lo), depth: 8 (over x, core).
Axes of the slice: x: 4, y: 4, z: 8 (z_hi: 2, z_lo: 4; z = z_hi * 4 + z_lo), core: 2. Of those that a mesh axis runs over, the one named last changes fastest.
Arguments:
- tokens: bfloat16 [4096, 6144], P(('col', 'depth'), 'row'), may hold values from -6 to 6
- w_in: bfloat16 [6144, 12288], P('row', 'col'), may hold values from -0.078125 to 0.078125
- w_out: bfloat16 [12288, 6144], P('col', 'row'), may hold values from -0.0546875 to 0.0546875
- grad_out: bfloat16 [4096, 6144], P(('col', 'depth'), 'row'), may hold values from -1.5 to 1.5
Outputs:
- output: bfloat16 [4096, 6144], P(('col', 'depth'), 'row')
- grad_tokens: bfloat16 [4096, 6144], P(('col', 'depth'), 'row')
- grad_w_in: bfloat16 [6144, 12288], P('row', ('col', 'depth'))
- grad_w_out: bfloat16 [12288, 6144], P(('col', 'depth'), 'row')
The draws below stay inside these ranges and needn't reach their ends.
All inputs are finite; a program needn't handle non-finite values.
Results may differ from the reference program's by a relative error of at most 0.029.
Values may be sent and summed in bfloat16 or wider, within the bound.
No kernel may reach another device: no remote copies, remote signals or barrier semaphores. Data moves between devices by JAX's collectives and lax.ppermute only.
A program may use at most 128 MiB of HBM per device.

```python
import jax
import jax.numpy as jnp
from jax import lax

D = 6144
FF = 12288
TOK_DEV = 128
TOKENS = 4096
N_COL = 4
N_DEPTH = 8


def shard_levels(own_key, dims, cuts, least, largest):
    def one(position, shards_of):
        heights = jax.random.uniform(jax.random.fold_in(jax.random.fold_in(own_key, 6), position), (shards_of,), jnp.float32, least / len(cuts), largest / len(cuts))
        return jnp.repeat(jnp.exp(heights), dims[position] // shards_of).reshape((-1,) + (1,) * (len(dims) - position - 1))

    factor_of = one(*cuts[0])
    for cut in cuts[1:]:
        factor_of = factor_of * one(*cut)
    return factor_of


def scatter_about(own_key, extent, scale, bound, split=(), held_as=jnp.bfloat16):
    entries = scale * jax.random.normal(own_key, extent, jnp.float32)
    if split:
        entries = entries * shard_levels(own_key, extent, split, -0.22, 0.18)
    return jnp.clip(entries, -bound, bound).astype(held_as)


def setup_inputs(seed: int = 0) -> dict:
    key_list = jax.random.split(jax.random.key(seed), 5)
    return {
        "tokens": scatter_about(key_list[0], (TOKENS, D), 1.0, 6.0, ((0, 32), (1, 8))),
        "w_in": scatter_about(key_list[1], (D, FF), D ** -0.5, 0.078125, ((0, 8), (1, 4))),
        "w_out": scatter_about(key_list[2], (FF, D), FF ** -0.5, 0.0546875, ((0, 4), (1, 8))),
        "grad_out": scatter_about(key_list[3], (TOKENS, D), 0.25, 1.5, ((0, 32), (1, 8))),
    }


def gelu_tanh(value):
    return jax.nn.gelu(value, approximate=True)

def reference(tokens, w_in, w_out, grad_out):
    pre = jnp.dot(tokens, w_in, preferred_element_type=jnp.float32)
    act_full, backward = jax.vjp(gelu_tanh, pre)
    act = act_full.astype(jnp.bfloat16)
    output = jnp.dot(act, w_out, preferred_element_type=jnp.float32).astype(jnp.bfloat16)
    grad_act = jnp.dot(grad_out, w_out.T, preferred_element_type=jnp.float32)
    grad_pre = backward(grad_act)[0].astype(jnp.bfloat16)
    grad_tokens = jnp.dot(grad_pre, w_in.T, preferred_element_type=jnp.float32).astype(jnp.bfloat16)

    def grouped(array):
        width = array.shape[1]
        shaped = array.reshape(N_COL, N_DEPTH, TOK_DEV, width)
        return jnp.transpose(shaped, (1, 0, 2, 3)).reshape(N_DEPTH, N_COL * TOK_DEV, width)

    def accumulate(carry, pieces):
        tok_g, gpre_g, act_g, gout_g = pieces
        part_in = lax.dot_general(tok_g, gpre_g, (((0,), (0,)), ((), ())), preferred_element_type=jnp.float32).astype(jnp.bfloat16)
        part_out = lax.dot_general(act_g, gout_g, (((0,), (0,)), ((), ())), preferred_element_type=jnp.float32).astype(jnp.bfloat16)
        part_in, part_out = lax.optimization_barrier((part_in, part_out))
        return ((carry[0] + part_in.astype(jnp.float32), carry[1] + part_out.astype(jnp.float32)), None)
    start = (jnp.zeros((D, FF), jnp.float32), jnp.zeros((FF, D), jnp.float32))
    sums, _ = lax.scan(accumulate, start, (grouped(tokens), grouped(grad_pre), grouped(act), grouped(grad_out)))
    return (output, grad_tokens, sums[0].astype(jnp.bfloat16), sums[1].astype(jnp.bfloat16))
```

```python
import jax
import jax.numpy as jnp
from jax import lax
from jax.sharding import Mesh, PartitionSpec as P

AXES = ("h", "y", "l", "x", "c")
BLOCK = 128
HALF = 64


def gelu_tanh(value):
    return jax.nn.gelu(value, approximate=True)


def dot(a, b, ca, cb):
    return lax.dot_general(a, b, (((ca,), (cb,)), ((), ())), preferred_element_type=jnp.float32)


def around_z(value, step):
    return lax.ppermute(value, ("h", "l"), [(i, (i + step) % 8) for i in range(8)])


def around_y(value, step):
    return lax.ppermute(value, "y", [(i, (i + step) % 4) for i in range(4)])


def gather_z(block):
    lower, upper = block[:HALF], block[HALF:]
    below = [[lower, upper]]
    above = [[lower, upper]]
    for step in range(1, 5):
        from_below = [around_z(below[-1][0], 1), None]
        from_above = [None, around_z(above[-1][1], -1)]
        if step < 4:
            from_below[1] = around_z(below[-1][1], 1)
            from_above[0] = around_z(above[-1][0], -1)
        below.append(from_below)
        above.append(from_above)
    parts = [[lower, upper], above[1], above[2], above[3], [below[4][0], above[4][1]]]
    parts += [below[3], below[2], below[1]]
    return jnp.concatenate([piece for pair in parts for piece in pair], axis=0).reshape(
        8, BLOCK, block.shape[1]
    )


def scatter_z(chunk):
    def send(value, step):
        return around_z(value.astype(jnp.bfloat16), step)

    far = chunk(4)
    up_lower = send(far[:HALF], 1)
    down_upper = send(far[HALF:], -1)
    near = chunk(3)
    up_upper = send(near[HALF:], 1)
    up_lower = send(near[:HALF] + up_lower.astype(jnp.float32), 1)
    near = chunk(5)
    down_lower = send(near[:HALF], -1)
    down_upper = send(near[HALF:] + down_upper.astype(jnp.float32), -1)
    for step in (2, 1):
        near = chunk(step)
        up_lower = send(near[:HALF] + up_lower.astype(jnp.float32), 1)
        up_upper = send(near[HALF:] + up_upper.astype(jnp.float32), 1)
        near = chunk(8 - step)
        down_lower = send(near[:HALF] + down_lower.astype(jnp.float32), -1)
        down_upper = send(near[HALF:] + down_upper.astype(jnp.float32), -1)
    own = chunk(0)
    lower = own[:HALF] + up_lower.astype(jnp.float32) + down_lower.astype(jnp.float32)
    upper = own[HALF:] + up_upper.astype(jnp.float32) + down_upper.astype(jnp.float32)
    return jnp.concatenate([lower, upper], axis=0).astype(jnp.bfloat16)


def scatter_y(part):
    from_below = around_y(part[2, :HALF], 1)
    from_above = around_y(part[2, HALF:], -1)
    below_upper = around_y(part[1, HALF:], 1)
    above_lower = around_y(part[3, :HALF], -1)
    below_lower = around_y(part[1, :HALF] + from_below, 1)
    above_upper = around_y(part[3, HALF:] + from_above, -1)
    f32 = lambda value: value.astype(jnp.float32)
    lower = f32(part[0, :HALF]) + f32(below_lower) + f32(above_lower)
    upper = f32(part[0, HALF:]) + f32(below_upper) + f32(above_upper)
    return jnp.concatenate([lower, upper], axis=0)


def gather_y(share):
    below = around_y(share, 1)
    above = around_y(share, -1)
    far_upper = around_y(below[HALF:], 1)
    far_lower = around_y(above[:HALF], -1)
    return jnp.concatenate([share, above, far_lower, far_upper, below], axis=0)


def body(tokens, w_in, w_out, grad_out):
    h, y, l = lax.axis_index("h"), lax.axis_index("y"), lax.axis_index("l")
    depth = lax.axis_index("x") * 2 + lax.axis_index("c")
    z = h * 4 + l
    width = tokens.shape[1]
    hidden = w_in.shape[1] // 2
    swap = [(0, 1), (1, 0)]

    rows = width // 8
    piece = lax.dynamic_slice(w_in, (depth * rows, (1 - h) * hidden), (rows, hidden))
    w_in_other = lax.all_gather(lax.ppermute(piece, "h", swap), ("x", "c"), axis=0, tiled=True)
    w_in_own = lax.dynamic_slice(w_in, (0, h * hidden), (width, hidden))
    rows = hidden // 8
    piece = lax.dynamic_slice(w_out, ((1 - h) * hidden + depth * rows, 0), (rows, width))
    w_out_other = lax.all_gather(lax.ppermute(piece, "h", swap), ("x", "c"), axis=0, tiled=True)
    w_out_own = lax.dynamic_slice(w_out, (h * hidden, 0), (hidden, width))

    def arrange(ring):
        def pick(half, slot):
            offset = (half * 4 + (l + y + slot) % 4 - z) % 8
            return lax.dynamic_index_in_dim(ring, offset, 0, keepdims=False)

        return [jnp.concatenate([pick(half, j) for j in range(4)], axis=0) for half in (h, 1 - h)]

    tok_own, tok_other = arrange(gather_z(tokens))
    pre_part = dot(tok_own, w_in_own, 1, 0) + dot(tok_other, w_in_other, 1, 0)
    pre_share = scatter_y(pre_part.astype(jnp.bfloat16).reshape(4, BLOCK, hidden))
    act_share, backward = jax.vjp(gelu_tanh, pre_share)
    act = gather_y(act_share.astype(jnp.bfloat16))

    gout_own, gout_other = arrange(gather_z(grad_out))
    gact_part = dot(gout_own, w_out_own, 1, 1) + dot(gout_other, w_out_other, 1, 1)
    gact_share = scatter_y(gact_part.astype(jnp.bfloat16).reshape(4, BLOCK, hidden))
    gpre = gather_y(backward(gact_share)[0].astype(jnp.bfloat16))

    def chunk_of(own, other):
        both = jnp.stack([own, other]).reshape(2, 4, BLOCK, width)

        def chunk(step):
            half = (((z + step) % 8) // 4 + h) % 2
            slot = (step - y) % 4
            return lax.dynamic_slice(both, (half, slot, 0, 0), (1, 1, BLOCK, width)).reshape(BLOCK, width)

        return chunk

    output = scatter_z(chunk_of(dot(act, w_out_own, 1, 0), dot(act, w_out_other, 1, 0)))
    grad_tokens = scatter_z(chunk_of(dot(gpre, w_in_own, 1, 1), dot(gpre, w_in_other, 1, 1)))

    def ordered(own, other):
        first = jnp.where(h == 0, own, other)
        second = jnp.where(h == 0, other, own)
        return first, second

    def back(piece):
        pairs = [(a * 4 + q * 2 + r, q * 4 + a * 2 + r) for a in range(2) for q in range(2) for r in range(2)]
        return lax.ppermute(piece, ("h", "x"), pairs)

    def sum_depth(stacked):
        return lax.psum_scatter(stacked, ("x", "c"), scatter_dimension=0, tiled=False)

    quarter = hidden // 4
    halves = [
        dot(half, gout, 0, 0).astype(jnp.bfloat16) for half in (act,) for gout in ordered(gout_own, gout_other)
    ]
    pieces = jnp.stack([half[j * quarter : (j + 1) * quarter] for half in halves for j in range(4)])
    grad_w_out = back(sum_depth(pieces))
    halves = [dot(tok, gpre, 0, 0).astype(jnp.bfloat16) for tok in ordered(tok_own, tok_other)]
    pieces = jnp.stack([half[:, j * quarter : (j + 1) * quarter] for half in halves for j in range(4)])
    grad_w_in = back(sum_depth(pieces))
    return output, grad_tokens, grad_w_in, grad_w_out


def solution(mesh):
    fine = Mesh(mesh.devices.reshape(2, 4, 4, 4, 2), AXES)
    placed = (
        P(("l", "x", "c"), ("h", "y")),
        P(("h", "y"), "l"),
        P("l", ("h", "y")),
        P(("l", "x", "c"), ("h", "y")),
    )
    return jax.shard_map(
        body,
        mesh=fine,
        in_specs=placed,
        out_specs=(
            P(("l", "x", "c"), ("h", "y")),
            P(("l", "x", "c"), ("h", "y")),
            P(("h", "y"), ("l", "x", "c")),
            P(("l", "x", "c"), ("h", "y")),
        ),
        check_vma=False,
    )
```

```python
import functools

import jax
import jax.numpy as jnp
from jax import lax
from jax.experimental import pallas as pl
from jax.experimental.pallas import tpu as pltpu
from jax.sharding import Mesh, PartitionSpec as P

AXES = ("h", "y", "l", "x", "c")
BLOCK = 128
HALF = 64
ROWS = 4 * BLOCK
TILE = 512
BF16 = jnp.bfloat16
F32 = jnp.float32
ANYWHERE = pl.BlockSpec(memory_space=pl.ANY)
VMEM_MIB = 60
SPLIT_OUT = True
SPLIT_TOK = True
SPLIT_ACT = False
SPLIT_GPRE = True
SPLIT_SUM_IN = True


def gelu_tanh(value):
    return jax.nn.gelu(value, approximate=True)


def around_z(value, step):
    return lax.ppermute(value, ("h", "l"), [(i, (i + step) % 8) for i in range(8)])


def around(value, axis, step):
    return lax.ppermute(value, axis, [(i, (i + step) % 4) for i in range(4)])


def other_core(value):
    return lax.ppermute(value, "c", [(0, 1), (1, 0)])


def swap_halves(piece):
    return lax.ppermute(piece, "h", [(0, 1), (1, 0)])


def give_back(piece, by_left):
    h, q = lax.axis_index("h"), lax.axis_index("x") // 2
    keep, send = jnp.where(h == 0, piece[0], piece[1]), jnp.where(h == 0, piece[1], piece[0])
    got = swap_halves(send)
    mine = jnp.where(h == q, keep, got)
    theirs = around(jnp.where(h == q, got, keep), "x", 2)
    return jnp.concatenate(
        [jnp.where(q == 0, mine, theirs), jnp.where(q == 0, theirs, mine)], axis=1 if by_left else 0
    )


def at(index, size):
    return pl.ds(pl.multiple_of(index * size, size), size)


def local_call(kernel, ins, outs, scratch, copies, flops):
    moved = sum(a.size * a.dtype.itemsize for a in ins) + sum(a.size * a.dtype.itemsize for a in outs)
    return pl.pallas_call(
        kernel,
        out_shape=outs,
        in_specs=[ANYWHERE] * len(ins),
        out_specs=[ANYWHERE] * len(outs),
        scratch_shapes=scratch + [pltpu.SemaphoreType.DMA((copies,))],
        compiler_params=pltpu.CompilerParams(vmem_limit_bytes=VMEM_MIB * 1024 * 1024),
        cost_estimate=pl.CostEstimate(flops=flops, bytes_accessed=moved, transcendentals=0),
    )(*ins)


class Copies:
    def __init__(self, sems):
        self.sems, self.count, self.open = sems, 0, []

    def start(self, source, target):
        copy = pltpu.make_async_copy(source, target, self.sems.at[self.count])
        copy.start()
        self.count += 1
        self.open.append(copy)
        return copy

    def split(self):
        taken, self.open = self.open, []
        return taken

    def wait(self):
        for copy in self.open:
            copy.wait()
        self.open = []


def multiply(left, right, result, transposed, ready, finish=None):
    for n in range(result.shape[1] // TILE):
        ready(n)
        part = slice(n * TILE, (n + 1) * TILE)
        if transposed:
            value = lax.dot_general(left[...], right[part, :], (((1,), (1,)), ((), ())), preferred_element_type=F32)
        else:
            value = jnp.dot(left[...], right[:, part], preferred_element_type=F32)
        result[:, part] = value.astype(BF16)
        if finish is not None:
            finish(n)


RING = (0, 1, 2, 3, -1, -2, -3)


def project_kernel(by_rows, *refs):
    blocks, (lower, upper, weight, other) = refs[:7], refs[7:11]
    chunks, full_x, full_w = refs[11:15], refs[15], refs[16]
    xs, ws, result, sems = refs[17:]
    h, l, y = lax.axis_index("h"), lax.axis_index("l"), lax.axis_index("y")
    z = h * 4 + l
    width = blocks[0].shape[1]
    hidden = ws.shape[0] if by_rows else ws.shape[1]
    copies = Copies(sems)
    for step, block in zip(RING, blocks):
        place = (z + step + 8) % 8
        copies.start(block, xs.at[at(place % 4, BLOCK), at(place // 4, width)])
    place = (z + 4) % 8
    copies.start(lower, xs.at[at((place % 4) * 2, HALF), at(place // 4, width)])
    copies.start(upper, xs.at[at((place % 4) * 2 + 1, HALF), at(place // 4, width)])
    lefts = copies.split()
    rights = []
    for n in range(hidden // TILE):
        part = slice(n * TILE, (n + 1) * TILE)
        source = at(h * (hidden // TILE) + n, TILE)
        if by_rows:
            copies.start(weight.at[source, :], ws.at[part, at(h, width)])
            copies.start(other.at[part, :], ws.at[part, at(1 - h, width)])
        else:
            copies.start(weight.at[:, source], ws.at[at(h, width), part])
            copies.start(other.at[:, part], ws.at[at(1 - h, width), part])
        rights.append(copies.split())
    for copy in lefts:
        copy.wait()
    copies.start(xs, full_x)

    def ready(n):
        for copy in rights[n]:
            copy.wait()
        part = slice(n * TILE, (n + 1) * TILE)
        if by_rows:
            copies.start(ws.at[part, :], full_w.at[part, :])
        else:
            copies.start(ws.at[:, part], full_w.at[:, part])

    def finish(n):
        part = slice(n * TILE, (n + 1) * TILE)
        for step, chunk in enumerate(chunks):
            copies.start(result.at[at((y + step) % 4, BLOCK), part], chunk.at[:, part])

    multiply(xs, ws, result, by_rows, ready, finish)
    copies.wait()


def project(ring, weight, other, by_rows):
    width = ring[0].shape[1]
    hidden = other.shape[0] if by_rows else other.shape[1]
    w_shape = (hidden, 2 * width) if by_rows else (2 * width, hidden)
    outs = [jax.ShapeDtypeStruct((BLOCK, hidden), BF16)] * 4
    outs += [jax.ShapeDtypeStruct((ROWS, 2 * width), BF16), jax.ShapeDtypeStruct(w_shape, BF16)]
    scratch = [pltpu.VMEM((ROWS, 2 * width), BF16), pltpu.VMEM(w_shape, BF16), pltpu.VMEM((ROWS, hidden), BF16)]
    got = local_call(
        functools.partial(project_kernel, by_rows), list(ring) + [weight, other], outs, scratch, 9 + 1 + 7 * (hidden // TILE),
        4 * ROWS * width * hidden,
    )
    return got[:4], got[4], got[5]


def load_rows(copies, sources, target, y):
    if len(sources) == 1:
        copies.start(sources[0], target)
    else:
        for step, source in enumerate(sources):
            copies.start(source, target.at[at((y + step) % 4, BLOCK), :])


def chunks_kernel(count, transposed, *refs):
    sources, weight, outs = refs[:count], refs[count], refs[count + 1 : -4]
    left, right, result, sems = refs[-4:]
    h, l, y = lax.axis_index("h"), lax.axis_index("l"), lax.axis_index("y")
    z = h * 4 + l
    width = result.shape[1] // 2
    copies = Copies(sems)
    load_rows(copies, sources, left, y)
    lefts = copies.split()
    rights = []
    for n in range(result.shape[1] // TILE):
        part = slice(n * TILE, (n + 1) * TILE)
        if transposed:
            rights.append(copies.start(weight.at[part, :], right.at[part, :]))
        else:
            rights.append(copies.start(weight.at[:, part], right.at[:, part]))
    copies.split()
    for copy in lefts:
        copy.wait()
    multiply(left, right, result, transposed, lambda n: rights[n].wait())
    if len(outs) == 1:
        for place in range(8):
            copies.start(
                result.at[at(place % 4, BLOCK), at(place // 4, width)], outs[0].at[at(place, BLOCK), :]
            )
        copies.wait()
        return
    for step, out in zip(RING, outs):
        place = (z + step + 8) % 8
        copies.start(result.at[at(place % 4, BLOCK), at(place // 4, width)], out)
    place = (z + 4) % 8
    for part in range(2):
        copies.start(result.at[at((place % 4) * 2 + part, HALF), at(place // 4, width)], outs[7 + part])
    copies.wait()


def chunks_of(sources, weight, transposed, split):
    columns = weight.shape[0] if transposed else weight.shape[1]
    inner = weight.shape[1] if transposed else weight.shape[0]
    outs = [jax.ShapeDtypeStruct((BLOCK, columns // 2), BF16)] * 7
    outs += [jax.ShapeDtypeStruct((HALF, columns // 2), BF16)] * 2
    if not split:
        outs = [jax.ShapeDtypeStruct((8 * BLOCK, columns // 2), BF16)]
    scratch = [pltpu.VMEM((ROWS, inner), BF16), pltpu.VMEM(weight.shape, BF16), pltpu.VMEM((ROWS, columns), BF16)]
    return local_call(
        functools.partial(chunks_kernel, len(sources), transposed), list(sources) + [weight], outs, scratch,
        len(sources) + 9 + columns // TILE, 2 * ROWS * inner * columns,
    )


def pieces_kernel(counts, cores, by_left, *refs):
    lefts, rights = refs[: counts[0]], refs[counts[0] : sum(counts)]
    out = refs[sum(counts)]
    left, right, result, sems = refs[sum(counts) + 1 :]
    y, x, c = lax.axis_index("y"), lax.axis_index("x"), lax.axis_index("c")
    copies = Copies(sems)
    load_rows(copies, lefts, left, y)
    load_rows(copies, rights, right, y)
    copies.wait()
    size = result.shape[-1]
    first = copies.count

    def sent(step):
        return pltpu.make_async_copy(result.at[step], out.at[step], sems.at[first + step])

    def piece(step, carry):
        if cores == "all":
            place, core = step // 2, step % 2
        else:
            place, core = (x + step) % 4, (1 - c if cores == "other" else c)
        wide, narrow = place // 2, (place % 2) * 2 + core
        for k in range(2):
            cut = at(k * 2 + wide, size)
            a, b = (left[:, at(narrow, size)], right[:, cut]) if by_left else (left[:, cut], right[:, at(narrow, size)])
            value = lax.dot_general(a, b, (((0,), (0,)), ((), ())), preferred_element_type=F32)
            result[step, k] = value.astype(BF16)
        sent(step).start()
        return carry

    def finish(step, carry):
        sent(step).wait()
        return carry

    lax.fori_loop(0, result.shape[0], piece, 0)
    lax.fori_loop(0, result.shape[0], finish, 0)


def pieces_of(lefts, rights, cores, by_left):
    shape = lambda sources: (ROWS, sources[0].shape[1])
    size = shape(lefts)[1] // 4
    count = 8 if cores == "all" else 4
    held = (count, 2, size, size)
    scratch = [pltpu.VMEM(shape(lefts), BF16), pltpu.VMEM(shape(rights), BF16), pltpu.VMEM(held, BF16)]
    (got,) = local_call(
        functools.partial(pieces_kernel, (len(lefts), len(rights)), cores, by_left),
        list(lefts) + list(rights), [jax.ShapeDtypeStruct(held, BF16)], scratch,
        len(lefts) + len(rights) + count, 4 * ROWS * count * size * size,
    )
    return got


def after(*values):
    return lax.optimization_barrier(values)


def ring_step(low, high):
    return around_z(low, 1), around_z(high, -1)


def ring_end(block, ring):
    below, above = [low for low, _ in ring], [high for _, high in ring]
    return [block] + above + below + [around_z(below[2][:HALF], 1), around_z(above[2][HALF:], -1)]


def scatter_z(chunks):
    if len(chunks) == 1:
        return lax.psum_scatter(chunks[0], ("h", "l"), scatter_dimension=0, tiled=True)
    f32 = lambda value: value.astype(F32)
    c0, c1, c2, c3, d1, d2, d3, lower, upper = chunks
    up = jnp.pad(f32(around_z(lower, 1)), ((0, HALF), (0, 0)))
    down = jnp.pad(f32(around_z(upper, -1)), ((HALF, 0), (0, 0)))
    for c, d in ((c3, d3), (c2, d2), (c1, d1)):
        up = f32(around_z((f32(c) + up).astype(BF16), 1))
        down = f32(around_z((f32(d) + down).astype(BF16), -1))
    return (f32(c0) + up + down).astype(BF16)


STEPS = (1, 2, -1)


def exchange_y(chunks):
    return [around(chunk, "y", step) for chunk, step in zip(chunks[1:], STEPS)]


def total(own, got):
    value = own.astype(F32)
    for piece in got:
        value = value + piece.astype(F32)
    return value


def gather_y(share, split):
    if not split:
        return [lax.all_gather(share, "y", axis=0, tiled=True)]
    return [share] + [around(share, "y", -step) for step in STEPS]


def gather_depth(piece):
    return lax.all_gather(piece, ("x", "c"), axis=0, tiled=True)


def sum_depth(lefts, rights, by_left):
    return lax.psum_scatter(
        pieces_of(lefts, rights, "all", by_left), ("x", "c"), scatter_dimension=0, tiled=False
    )


def sum_cores(lefts, rights, by_left):
    theirs = other_core(pieces_of(lefts, rights, "other", by_left))
    mine = pieces_of(lefts, rights, "mine", by_left)
    own = mine[0].astype(F32) + theirs[0].astype(F32)
    return own, [(mine[k].astype(F32) + theirs[k].astype(F32)).astype(BF16) for k in (1, 2, 3)]


def sum_x(own, chunks):
    return total(own, [around(chunk, "x", step) for chunk, step in zip(chunks, STEPS)]).astype(BF16)


def body(tokens, w_in, w_out, grad_out):
    h = lax.axis_index("h")
    depth = lax.axis_index("x") * 2 + lax.axis_index("c")
    width = tokens.shape[1]
    hidden = w_in.shape[1] // 2

    rows = width // 8
    piece_in = lax.dynamic_slice(w_in, (depth * rows, (1 - h) * hidden), (rows, hidden))
    rows = hidden // 8
    piece_out = lax.dynamic_slice(w_out, ((1 - h) * hidden + depth * rows, 0), (rows, width))

    piece_in = swap_halves(piece_in)
    ring = [ring_step(tokens, tokens)]
    ring[0], piece_out = after(ring[0], piece_out)
    piece_out = swap_halves(piece_out)
    ring.append(ring_step(*ring[0]))
    ring[1], piece_in = after(ring[1], piece_in)
    w_in_other = gather_depth(piece_in)
    ring.append(ring_step(*ring[1]))
    blocks, piece_out, grad_out = after(ring_end(tokens, ring), piece_out, grad_out)
    w_out_other = gather_depth(piece_out)

    ring = [ring_step(grad_out, grad_out)]
    ring.append(ring_step(*ring[0]))
    ring[1], w_in_other = after(ring[1], w_in_other)
    chunks, tok, w_in_full = project(blocks, w_in, w_in_other, False)
    ring[1], chunks = after(ring[1], chunks)
    got = exchange_y(chunks)
    ring.append(ring_step(*ring[1]))
    blocks = ring_end(grad_out, ring)
    got, blocks = after(got, blocks)
    pre_share = total(chunks[0], got)
    act_share, pre_share, blocks = after(gelu_tanh(pre_share).astype(BF16), pre_share, blocks)
    act = gather_y(act_share, SPLIT_ACT)

    chunks, gout, w_out_full = project(blocks, w_out, w_out_other, True)
    got = exchange_y(chunks)
    gact_share = total(chunks[0], got)
    _, backward = jax.vjp(gelu_tanh, pre_share)
    gpre_share = backward(gact_share)[0].astype(BF16)
    gpre_share, act = after(gpre_share, act)
    gpre = gather_y(gpre_share, SPLIT_GPRE)

    sum_out = sum_depth(act, [gout], True)
    out_chunks = chunks_of(act, w_out_full, False, SPLIT_OUT)
    output = scatter_z(out_chunks)
    out_chunks, gpre = after(out_chunks, gpre)
    if SPLIT_SUM_IN:
        own, chunks = sum_cores([tok], gpre, False)
        chunks, gpre = after(chunks, gpre)
        sum_in = sum_x(own, chunks)
    else:
        sum_in = sum_depth([tok], gpre, False)
    tok_chunks = chunks_of(gpre, w_in_full, True, SPLIT_TOK)
    grad_tokens = scatter_z(tok_chunks)
    grad_w_out = give_back(sum_out, True)
    grad_w_in = give_back(sum_in, False)
    return output, grad_tokens, grad_w_in, grad_w_out


def solution(mesh):
    fine = Mesh(mesh.devices.reshape(2, 4, 4, 4, 2), AXES)
    block = P(("l", "x", "c"), ("h", "y"))
    return jax.shard_map(
        body,
        mesh=fine,
        in_specs=(block, P(("h", "y"), "l"), P("l", ("h", "y")), block),
        out_specs=(block, block, P(("h", "y"), ("l", "x", "c")), block),
        check_vma=False,
    )
```

```python
import functools

import jax
import jax.numpy as jnp
from jax import lax
from jax.experimental import pallas as pl
from jax.experimental.pallas import tpu as pltpu
from jax.sharding import Mesh, PartitionSpec as P

AXES = ("h", "y", "l", "x", "c")
BLOCK = 128
HALF = 64
ROWS = 4 * BLOCK
TILE = 512
BF16 = jnp.bfloat16
F32 = jnp.float32
ANYWHERE = pl.BlockSpec(memory_space=pl.ANY)
VMEM_MIB = 60
SCALE = 1000
SWAP_EARLY = False
SPLIT_TOK = False


def gelu_tanh(value):
    return jax.nn.gelu(value, approximate=True)


def around_z(value, step):
    return lax.ppermute(value, ("h", "l"), [(i, (i + step) % 8) for i in range(8)])


def around(value, axis, step):
    return lax.ppermute(value, axis, [(i, (i + step) % 4) for i in range(4)])


def other_core(value):
    return lax.ppermute(value, "c", [(0, 1), (1, 0)])


def swap_halves(piece):
    return lax.ppermute(piece, "h", [(0, 1), (1, 0)])


def give_z(piece):
    h, q = lax.axis_index("h"), lax.axis_index("x") // 2
    keep, send = jnp.where(h == 0, piece[0], piece[1]), jnp.where(h == 0, piece[1], piece[0])
    got = swap_halves(send)
    return jnp.where(h == q, keep, got), jnp.where(h == q, got, keep)


def give_x(mine, theirs, by_left):
    q = lax.axis_index("x") // 2
    theirs = around(theirs, "x", 2)
    return jnp.concatenate(
        [jnp.where(q == 0, mine, theirs), jnp.where(q == 0, theirs, mine)], axis=1 if by_left else 0
    )


def at(index, size):
    return pl.ds(pl.multiple_of(index * size, size), size)


def local_call(kernel, ins, outs, scratch, copies, flops):
    moved = sum(a.size * a.dtype.itemsize for a in ins) + sum(a.size * a.dtype.itemsize for a in outs)
    return pl.pallas_call(
        kernel,
        out_shape=outs,
        in_specs=[ANYWHERE] * len(ins),
        out_specs=[ANYWHERE] * len(outs),
        scratch_shapes=scratch + [pltpu.SemaphoreType.DMA((copies,))],
        compiler_params=pltpu.CompilerParams(vmem_limit_bytes=VMEM_MIB * 1024 * 1024),
        cost_estimate=pl.CostEstimate(flops=flops // SCALE, bytes_accessed=moved // SCALE, transcendentals=0),
    )(*ins)


class Copies:
    def __init__(self, sems):
        self.sems, self.count, self.open = sems, 0, []

    def start(self, source, target):
        copy = pltpu.make_async_copy(source, target, self.sems.at[self.count])
        copy.start()
        self.count += 1
        self.open.append(copy)
        return copy

    def split(self):
        taken, self.open = self.open, []
        return taken

    def wait(self):
        for copy in self.open:
            copy.wait()
        self.open = []


def multiply(left, right, result, transposed, finish=None):
    for n in range(result.shape[1] // TILE):
        part = slice(n * TILE, (n + 1) * TILE)
        if transposed:
            value = lax.dot_general(left[...], right[part, :], (((1,), (1,)), ((), ())), preferred_element_type=F32)
        else:
            value = jnp.dot(left[...], right[:, part], preferred_element_type=F32)
        result[:, part] = value.astype(BF16)
        if finish is not None:
            finish(n)


RING = (0, 1, 2, 3, -1, -2, -3)


def load_weights(copies, weight, others, target, by_rows):
    h, x, c = lax.axis_index("h"), lax.axis_index("x"), lax.axis_index("c")
    width = weight.shape[1] if by_rows else weight.shape[0]
    rows = others[0].shape[0] // 4
    if len(others) == 1:
        copies.start(others[0], target.at[:, at(1 - h, width)] if by_rows else target.at[at(1 - h, width), :])
    else:
        for pieces, core in zip(others, (c, 1 - c)):
            for step in range(4):
                place = ((x + step) % 4) * 2 + core
                source = pieces.at[step * rows : (step + 1) * rows, :]
                if by_rows:
                    copies.start(source, target.at[at(place, rows), at(1 - h, width)])
                else:
                    copies.start(source, target.at[at((1 - h) * 8 + place, rows), :])
    if by_rows:
        copies.start(weight.at[at(h, target.shape[0]), :], target.at[:, at(h, width)])
    else:
        copies.start(weight.at[:, at(h, target.shape[1])], target.at[at(h, width), :])


def project_kernel(by_rows, count, *refs):
    blocks, (lower, upper, weight) = refs[:7], refs[7:10]
    others, chunks, full_x = refs[10 : 10 + count], refs[10 + count : -5], refs[-5]
    xs, ws, result, sems = refs[-4:]
    h, l, y = lax.axis_index("h"), lax.axis_index("l"), lax.axis_index("y")
    z = h * 4 + l
    width = blocks[0].shape[1]
    copies = Copies(sems)
    load_weights(copies, weight, others, ws, by_rows)
    for step, block in zip(RING, blocks):
        place = (z + step + 8) % 8
        copies.start(block, xs.at[at(place % 4, BLOCK), at(place // 4, width)])
    place = (z + 4) % 8
    copies.start(lower, xs.at[at((place % 4) * 2, HALF), at(place // 4, width)])
    copies.start(upper, xs.at[at((place % 4) * 2 + 1, HALF), at(place // 4, width)])
    copies.wait()
    copies.start(xs, full_x)

    def finish(n):
        part = slice(n * TILE, (n + 1) * TILE)
        for step, chunk in enumerate(chunks):
            copies.start(result.at[at((y + step) % 4, BLOCK), part], chunk.at[:, part])

    multiply(xs, ws, result, by_rows, finish)
    copies.wait()


def weights_shape(weight, by_rows):
    rows, columns = weight.shape
    return (rows // 2, columns * 2) if by_rows else (rows * 2, columns // 2)


def project(ring, weight, others, by_rows):
    w_shape = weights_shape(weight, by_rows)
    inner, hidden = w_shape[::-1] if by_rows else w_shape
    outs = [jax.ShapeDtypeStruct((BLOCK, hidden), BF16)] * 4 + [jax.ShapeDtypeStruct((ROWS, inner), BF16)]
    scratch = [pltpu.VMEM((ROWS, inner), BF16), pltpu.VMEM(w_shape, BF16), pltpu.VMEM((ROWS, hidden), BF16)]
    got = local_call(
        functools.partial(project_kernel, by_rows, len(others)), list(ring) + [weight] + list(others), outs, scratch,
        19 + 4 * (hidden // TILE), 2 * ROWS * inner * hidden,
    )
    return got[:-1], got[-1]


def load_rows(copies, sources, target, y):
    if len(sources) == 1:
        copies.start(sources[0], target)
    else:
        for step, source in enumerate(sources):
            copies.start(source, target.at[at((y + step) % 4, BLOCK), :])


def chunks_kernel(count, extra, by_rows, *refs):
    sources, weight, others = refs[:count], refs[count], refs[count + 1 : count + 1 + extra]
    outs = refs[count + 1 + extra : -4]
    left, right, result, sems = refs[-4:]
    y = lax.axis_index("y")
    width = result.shape[1] // 2
    copies = Copies(sems)
    load_rows(copies, sources, left, y)
    load_weights(copies, weight, others, right, by_rows)
    copies.wait()
    multiply(left, right, result, not by_rows)
    if len(outs) == 1:
        for place in range(8):
            copies.start(
                result.at[at(place % 4, BLOCK), at(place // 4, width)], outs[0].at[at(place, BLOCK), :]
            )
        copies.wait()
        return
    cut_z(copies, result, outs)
    copies.wait()


def cut_z(copies, result, outs):
    z = lax.axis_index("h") * 4 + lax.axis_index("l")
    width = result.shape[1] // 2
    for step, out in zip(RING, outs):
        place = (z + step + 8) % 8
        copies.start(result.at[at(place % 4, BLOCK), at(place // 4, width)], out)
    place = (z + 4) % 8
    for part in range(2):
        copies.start(result.at[at((place % 4) * 2 + part, HALF), at(place // 4, width)], outs[7 + part])


def chunks_of(sources, weight, others, by_rows, split):
    w_shape = weights_shape(weight, by_rows)
    inner, columns = w_shape if by_rows else w_shape[::-1]
    outs = [jax.ShapeDtypeStruct((BLOCK, columns // 2), BF16)] * 7
    outs += [jax.ShapeDtypeStruct((HALF, columns // 2), BF16)] * 2
    if not split:
        outs = [jax.ShapeDtypeStruct((8 * BLOCK, columns // 2), BF16)]
    scratch = [pltpu.VMEM((ROWS, inner), BF16), pltpu.VMEM(w_shape, BF16), pltpu.VMEM((ROWS, columns), BF16)]
    return local_call(
        functools.partial(chunks_kernel, len(sources), len(others), by_rows),
        list(sources) + [weight] + list(others), outs, scratch, len(sources) + 18, 2 * ROWS * inner * columns,
    )


def pieces_kernel(counts, cores, by_left, *refs):
    lefts, rights = refs[: counts[0]], refs[counts[0] : sum(counts)]
    outs = refs[sum(counts) : -5]
    left, right, turned, result, sems = refs[-5:]
    y = lax.axis_index("y")
    copies = Copies(sems)
    load_rows(copies, lefts, left, y)
    load_rows(copies, rights, right, y)
    copies.wait()
    make_pieces(copies, left, right, turned, result, outs, cores, by_left)
    copies.wait()


def make_pieces(copies, left, right, turned, result, outs, cores, by_left):
    x, c = lax.axis_index("x"), lax.axis_index("c")
    size = result.shape[-1]
    for n in range(4):
        part = slice(n * size, (n + 1) * size)
        turned[part, :] = left[:, part].T

    def piece(step, carry):
        r = step % 2
        core = step // 2 if cores == "all" else jnp.where(step < 2, 1 - c, c)
        narrow = r * 2 + core
        if by_left:
            value = jnp.dot(turned[at(narrow, size), :], right[...], preferred_element_type=F32).astype(BF16)
        else:
            value = jnp.dot(turned[...], right[:, at(narrow, size)], preferred_element_type=F32).astype(BF16)
        for q in range(2):
            place = q * 2 + r
            slot = place * 2 + core if cores == "all" else (step // 2) * 4 + (place - x + 4) % 4
            for k in range(2):
                part = slice((k * 2 + q) * size, (k * 2 + q + 1) * size)
                result[slot, k] = value[:, part] if by_left else value[part, :]
        return carry

    if len(outs) == 1:
        whole = [(0, 4, outs[0])]
    else:
        whole = [(0, 2, outs[0]), (2, 4, outs[1])]
    for begin, end, out in whole:
        lax.fori_loop(begin, end, piece, 0)
        copies.start(result.at[begin * 2 : end * 2], out)


def both_kernel(count, extra, *refs):
    sources, right_source, weight = refs[:count], refs[count], refs[count + 1]
    others, outs = refs[count + 2 : count + 2 + extra], refs[count + 2 + extra : -8]
    left, right, turned, pieces, held, result, sems, more = refs[-8:]
    y = lax.axis_index("y")
    copies, late = Copies(sems), Copies(more)
    load_rows(copies, sources, left, y)
    copies.start(right_source, right)
    load_weights(late, weight, others, held, True)
    copies.wait()
    make_pieces(copies, left, right, turned, pieces, outs[:1], "all", True)
    late.wait()
    multiply(left, held, result, False)
    cut_z(copies, result, outs[1:])
    copies.wait()


def both_of(sources, right, weight, others):
    w_shape = weights_shape(weight, True)
    hidden, width = w_shape
    size = hidden // 4
    outs = [jax.ShapeDtypeStruct((8, 2, size, size), BF16)] + [jax.ShapeDtypeStruct((BLOCK, width // 2), BF16)] * 7
    outs += [jax.ShapeDtypeStruct((HALF, width // 2), BF16)] * 2
    scratch = [
        pltpu.VMEM((ROWS, hidden), BF16), pltpu.VMEM((ROWS, width), BF16), pltpu.VMEM((hidden, ROWS), BF16),
        pltpu.VMEM((8, 2, size, size), BF16), pltpu.VMEM(w_shape, BF16), pltpu.VMEM((ROWS, width), BF16),
        pltpu.SemaphoreType.DMA((len(sources) + 11,)),
    ]
    got = local_call(
        functools.partial(both_kernel, len(sources), len(others)),
        list(sources) + [right, weight] + list(others), outs, scratch, 9, 4 * ROWS * hidden * width,
    )
    return got[0], list(got[1:])


def pieces_of(lefts, rights, cores, by_left):
    shape = lambda sources: (ROWS, sources[0].shape[1])
    size = shape(lefts)[1] // 4
    held = (8, 2, size, size)
    scratch = [pltpu.VMEM(shape(lefts), BF16), pltpu.VMEM(shape(rights), BF16)]
    scratch += [pltpu.VMEM(shape(lefts)[::-1], BF16), pltpu.VMEM(held, BF16)]
    parts = 1 if cores == "all" else 2
    outs = [jax.ShapeDtypeStruct((8 // parts, 2, size, size), BF16)] * parts
    return local_call(
        functools.partial(pieces_kernel, (len(lefts), len(rights)), cores, by_left),
        list(lefts) + list(rights), outs, scratch, len(lefts) + len(rights) + parts, 32 * ROWS * size * size,
    )


def after(*values):
    return lax.optimization_barrier(values)


def ring_step(low, high):
    return around_z(low, 1), around_z(high, -1)


def ring_end(block, ring):
    below, above = [low for low, _ in ring], [high for _, high in ring]
    return [block] + above + below + [around_z(below[2][:HALF], 1), around_z(above[2][HALF:], -1)]


def scatter_begin(chunks):
    f32 = lambda value: value.astype(F32)
    up = jnp.pad(f32(around_z(chunks[7], 1)), ((0, HALF), (0, 0)))
    down = jnp.pad(f32(around_z(chunks[8], -1)), ((HALF, 0), (0, 0)))
    return (f32(chunks[3]) + up).astype(BF16), (f32(chunks[6]) + down).astype(BF16)


def scatter_step(state, chunks, step):
    up, down = around_z(state[0], 1).astype(F32), around_z(state[1], -1).astype(F32)
    if step == 0:
        return (chunks[0].astype(F32) + up + down).astype(BF16)
    return (chunks[step].astype(F32) + up).astype(BF16), (chunks[3 + step].astype(F32) + down).astype(BF16)


def scatter_z(chunks):
    if len(chunks) == 1:
        return lax.psum_scatter(chunks[0], ("h", "l"), scatter_dimension=0, tiled=True)
    state = scatter_begin(chunks)
    for step in (2, 1, 0):
        state = scatter_step(state, chunks, step)
    return state


STEPS = (1, 2, -1)


def exchange_y(chunks):
    return [around(chunk, "y", step) for chunk, step in zip(chunks[1:], STEPS)]


def total(own, got):
    value = own.astype(F32)
    for piece in got:
        value = value + piece.astype(F32)
    return value


def gather_y(share):
    return [share] + [around(share, "y", -step) for step in STEPS]


def gather_x(piece):
    got = [around(piece, "x", -step) for step in STEPS]
    return jnp.concatenate([piece] + got, axis=0)


def body(tokens, w_in, w_out, grad_out):
    h = lax.axis_index("h")
    depth = lax.axis_index("x") * 2 + lax.axis_index("c")
    width = tokens.shape[1]
    hidden = w_in.shape[1] // 2

    rows = width // 8
    piece_in = lax.dynamic_slice(w_in, (depth * rows, (1 - h) * hidden), (rows, hidden))
    rows = hidden // 8
    piece_out = lax.dynamic_slice(w_out, ((1 - h) * hidden + depth * rows, 0), (rows, width))

    piece_in = swap_halves(piece_in)
    ring = [ring_step(tokens, tokens)]
    ring[0], piece_in = after(ring[0], piece_in)
    mine_in = gather_x(piece_in)
    if SWAP_EARLY:
        ring[0], piece_out = after(ring[0], piece_out)
    ring.append(ring_step(*ring[0]))
    if not SWAP_EARLY:
        ring[1], piece_out = after(ring[1], piece_out)
    piece_out = swap_halves(piece_out)
    ring.append(ring_step(*ring[1]))
    ring[2], mine_in = after(ring[2], mine_in)
    theirs_in = other_core(mine_in)
    blocks, theirs_in, piece_out, grad_out = after(ring_end(tokens, ring), theirs_in, piece_out, grad_out)
    w_out_others = [lax.all_gather(piece_out, ("x", "c"), axis=0, tiled=True)]
    w_in_others = [mine_in, theirs_in]

    ring = [ring_step(grad_out, grad_out)]
    pre_chunks, tok = project(blocks, w_in, w_in_others, False)
    pre_chunks, ring[0] = after(pre_chunks, ring[0])
    got = exchange_y(pre_chunks)
    ring.append(ring_step(*ring[0]))
    ring.append(ring_step(*ring[1]))
    got, blocks = after(got, ring_end(grad_out, ring))
    pre_share = total(pre_chunks[0], got)
    act_share, pre_share, blocks = after(gelu_tanh(pre_share).astype(BF16), pre_share, blocks)
    act = gather_y(act_share)

    chunks, gout = project(blocks, w_out, w_out_others, True)
    act, chunks = after(act, chunks)
    got = exchange_y(chunks)
    pieces, out_chunks = both_of(act, gout, w_out, w_out_others)
    got, out_chunks, pieces = after(got, out_chunks, pieces)
    sum_out = lax.psum_scatter(pieces, ("x", "c"), scatter_dimension=0, tiled=False)
    gact_share = total(chunks[0], got)
    _, backward = jax.vjp(gelu_tanh, pre_share)
    gpre_share = backward(gact_share)[0].astype(BF16)
    gpre = gather_y(gpre_share)
    state = scatter_begin(out_chunks)
    state = scatter_step(state, out_chunks, 2)
    gpre, state = after(gpre, state)

    theirs, mine = pieces_of([tok], gpre, "each", False)
    gpre, mine = after(gpre, mine)
    theirs = other_core(theirs)
    tok_chunks = chunks_of(gpre, w_in, w_in_others, False, SPLIT_TOK)
    theirs, mine, tok_chunks = after(theirs, mine, tok_chunks)
    halves = [mine[k].astype(F32) + theirs[k].astype(F32) for k in range(4)]
    sends = [jnp.where(h == 0, half[1], half[0]) for half in halves]
    keeps = [jnp.where(h == 0, half[0], half[1]) for half in halves]
    sends, keeps = after([sends[0]] + [v.astype(BF16) for v in sends[1:]], [keeps[0]] + [v.astype(BF16) for v in keeps[1:]])
    got = [around(chunk, "x", step) for chunk, step in zip(sends[1:], STEPS)]
    state = scatter_step(state, out_chunks, 1)
    swapped = give_z(sum_out)
    got, keeps, state, swapped = after(got, keeps, state, swapped)
    received = swap_halves(total(sends[0], got).astype(BF16))
    got = [around(chunk, "x", step) for chunk, step in zip(keeps[1:], STEPS)]
    kept = total(keeps[0], got).astype(BF16)
    output = scatter_step(state, out_chunks, 0)
    grad_tokens = scatter_z(tok_chunks)
    grad_w_out = give_x(*swapped, True)
    q = lax.axis_index("x") // 2
    grad_w_in = give_x(jnp.where(h == q, kept, received), jnp.where(h == q, received, kept), False)
    return output, grad_tokens, grad_w_in, grad_w_out


def solution(mesh):
    fine = Mesh(mesh.devices.reshape(2, 4, 4, 4, 2), AXES)
    block = P(("l", "x", "c"), ("h", "y"))
    return jax.shard_map(
        body,
        mesh=fine,
        in_specs=(block, P(("h", "y"), "l"), P("l", ("h", "y")), block),
        out_specs=(block, block, P(("h", "y"), ("l", "x", "c")), block),
        check_vma=False,
    )
```

```python
import functools

import jax
import jax.numpy as jnp
from jax import lax
from jax.experimental import pallas as pl
from jax.experimental.pallas import tpu as pltpu
from jax.sharding import Mesh, PartitionSpec as P

AXES = ("h", "y", "l", "x", "c")
BLOCK = 128
HALF = 64
ROWS = 4 * BLOCK
TILE = 512
BF16 = jnp.bfloat16
F32 = jnp.float32
ANYWHERE = pl.BlockSpec(memory_space=pl.ANY)
VMEM_MIB = 60
SCALE = 1000
SPLIT_TOK = False
TIE_ACT = False
TIE_KEEP = True


def gelu_tanh(value):
    return jax.nn.gelu(value, approximate=True)


def around_z(value, step):
    return lax.ppermute(value, ("h", "l"), [(i, (i + step) % 8) for i in range(8)])


def around(value, axis, step):
    return lax.ppermute(value, axis, [(i, (i + step) % 4) for i in range(4)])


def other_core(value):
    return lax.ppermute(value, "c", [(0, 1), (1, 0)])


def swap_halves(piece):
    return lax.ppermute(piece, "h", [(0, 1), (1, 0)])


def give_z(piece):
    h, q = lax.axis_index("h"), lax.axis_index("x") // 2
    keep, send = jnp.where(h == 0, piece[0], piece[1]), jnp.where(h == 0, piece[1], piece[0])
    got = swap_halves(send)
    return jnp.where(h == q, keep, got), jnp.where(h == q, got, keep)


def give_x(mine, theirs, by_left):
    q = lax.axis_index("x") // 2
    theirs = around(theirs, "x", 2)
    return jnp.concatenate(
        [jnp.where(q == 0, mine, theirs), jnp.where(q == 0, theirs, mine)], axis=1 if by_left else 0
    )


def at(index, size):
    return pl.ds(pl.multiple_of(index * size, size), size)


def local_call(kernel, ins, outs, scratch, copies, flops):
    moved = sum(a.size * a.dtype.itemsize for a in ins) + sum(a.size * a.dtype.itemsize for a in outs)
    return pl.pallas_call(
        kernel,
        out_shape=outs,
        in_specs=[ANYWHERE] * len(ins),
        out_specs=[ANYWHERE] * len(outs),
        scratch_shapes=scratch + [pltpu.SemaphoreType.DMA((copies,))],
        compiler_params=pltpu.CompilerParams(vmem_limit_bytes=VMEM_MIB * 1024 * 1024),
        cost_estimate=pl.CostEstimate(flops=flops // SCALE, bytes_accessed=moved // SCALE, transcendentals=0),
    )(*ins)


class Copies:
    def __init__(self, sems):
        self.sems, self.count, self.open = sems, 0, []

    def start(self, source, target):
        copy = pltpu.make_async_copy(source, target, self.sems.at[self.count])
        copy.start()
        self.count += 1
        self.open.append(copy)
        return copy

    def split(self):
        taken, self.open = self.open, []
        return taken

    def wait(self):
        for copy in self.open:
            copy.wait()
        self.open = []


def multiply(left, right, result, transposed, finish=None, ready=None):
    for n in range(result.shape[1] // TILE):
        part = slice(n * TILE, (n + 1) * TILE)
        if ready is not None:
            ready(n)
        if transposed:
            value = lax.dot_general(left[...], right[part, :], (((1,), (1,)), ((), ())), preferred_element_type=F32)
        else:
            value = jnp.dot(left[...], right[:, part], preferred_element_type=F32)
        result[:, part] = value.astype(BF16)
        if finish is not None:
            finish(n)


RING = (0, 1, 2, 3, -1, -2, -3)


def load_weights(copies, weight, others, target, by_rows):
    h, x, c = lax.axis_index("h"), lax.axis_index("x"), lax.axis_index("c")
    width = weight.shape[1] if by_rows else weight.shape[0]
    rows = others[0].shape[0] // 4
    if len(others) == 1:
        copies.start(others[0], target.at[:, at(1 - h, width)] if by_rows else target.at[at(1 - h, width), :])
    else:
        for pieces, core in zip(others, (c, 1 - c)):
            for step in range(4):
                place = ((x + step) % 4) * 2 + core
                source = pieces.at[step * rows : (step + 1) * rows, :]
                if by_rows:
                    copies.start(source, target.at[at(place, rows), at(1 - h, width)])
                else:
                    copies.start(source, target.at[at((1 - h) * 8 + place, rows), :])
    if by_rows:
        copies.start(weight.at[at(h, target.shape[0]), :], target.at[:, at(h, width)])
    else:
        copies.start(weight.at[:, at(h, target.shape[1])], target.at[at(h, width), :])


def load_tiles(copies, weight, others, target, by_rows):
    h, x, c = lax.axis_index("h"), lax.axis_index("x"), lax.axis_index("c")
    tiles = target.shape[0 if by_rows else 1] // TILE
    width = weight.shape[1] if by_rows else weight.shape[0]
    rows = others[0].shape[0] // 4
    taken = []
    for n in range(tiles):
        part, source = slice(n * TILE, (n + 1) * TILE), at(h * tiles + n, TILE)
        if by_rows:
            copies.start(weight.at[source, :], target.at[part, at(h, width)])
            copies.start(others[0].at[part, :], target.at[part, at(1 - h, width)])
        else:
            copies.start(weight.at[:, source], target.at[at(h, width), part])
            for pieces, core in zip(others, (c, 1 - c)):
                for step in range(4):
                    place = (1 - h) * 8 + ((x + step) % 4) * 2 + core
                    copies.start(pieces.at[step * rows : (step + 1) * rows, part], target.at[at(place, rows), part])
        taken.append(copies.split())
    return taken


def project_kernel(by_rows, count, *refs):
    blocks, (lower, upper, weight) = refs[:7], refs[7:10]
    others, chunks, full_x = refs[10 : 10 + count], refs[10 + count : -5], refs[-5]
    xs, ws, result, sems = refs[-4:]
    h, l, y = lax.axis_index("h"), lax.axis_index("l"), lax.axis_index("y")
    z = h * 4 + l
    width = blocks[0].shape[1]
    copies = Copies(sems)
    for step, block in zip(RING, blocks):
        place = (z + step + 8) % 8
        copies.start(block, xs.at[at(place % 4, BLOCK), at(place // 4, width)])
    place = (z + 4) % 8
    copies.start(lower, xs.at[at((place % 4) * 2, HALF), at(place // 4, width)])
    copies.start(upper, xs.at[at((place % 4) * 2 + 1, HALF), at(place // 4, width)])
    lefts = copies.split()
    tiles = load_tiles(copies, weight, others, ws, by_rows)
    for copy in lefts:
        copy.wait()
    copies.start(xs, full_x)

    def ready(n):
        for copy in tiles[n]:
            copy.wait()

    def finish(n):
        part = slice(n * TILE, (n + 1) * TILE)
        for step, chunk in enumerate(chunks):
            copies.start(result.at[at((y + step) % 4, BLOCK), part], chunk.at[:, part])

    multiply(xs, ws, result, by_rows, finish, ready)
    copies.wait()


def weights_shape(weight, by_rows):
    rows, columns = weight.shape
    return (rows // 2, columns * 2) if by_rows else (rows * 2, columns // 2)


def project(ring, weight, others, by_rows):
    w_shape = weights_shape(weight, by_rows)
    inner, hidden = w_shape[::-1] if by_rows else w_shape
    outs = [jax.ShapeDtypeStruct((BLOCK, hidden), BF16)] * 4 + [jax.ShapeDtypeStruct((ROWS, inner), BF16)]
    scratch = [pltpu.VMEM((ROWS, inner), BF16), pltpu.VMEM(w_shape, BF16), pltpu.VMEM((ROWS, hidden), BF16)]
    got = local_call(
        functools.partial(project_kernel, by_rows, len(others)), list(ring) + [weight] + list(others), outs, scratch,
        10 + 13 * (hidden // TILE), 2 * ROWS * inner * hidden,
    )
    return got[:-1], got[-1]


def load_rows(copies, sources, target, y):
    if len(sources) == 1:
        copies.start(sources[0], target)
    else:
        for step, source in enumerate(sources):
            copies.start(source, target.at[at((y + step) % 4, BLOCK), :])


def chunks_kernel(count, extra, by_rows, *refs):
    sources, weight, others = refs[:count], refs[count], refs[count + 1 : count + 1 + extra]
    outs = refs[count + 1 + extra : -4]
    left, right, result, sems = refs[-4:]
    y = lax.axis_index("y")
    width = result.shape[1] // 2
    copies = Copies(sems)
    load_rows(copies, sources, left, y)
    load_weights(copies, weight, others, right, by_rows)
    copies.wait()
    multiply(left, right, result, not by_rows)
    if len(outs) == 1:
        for place in range(8):
            copies.start(
                result.at[at(place % 4, BLOCK), at(place // 4, width)], outs[0].at[at(place, BLOCK), :]
            )
        copies.wait()
        return
    cut_z(copies, result, outs)
    copies.wait()


def cut_z(copies, result, outs):
    z = lax.axis_index("h") * 4 + lax.axis_index("l")
    width = result.shape[1] // 2
    for step, out in zip(RING, outs):
        place = (z + step + 8) % 8
        copies.start(result.at[at(place % 4, BLOCK), at(place // 4, width)], out)
    place = (z + 4) % 8
    for part in range(2):
        copies.start(result.at[at((place % 4) * 2 + part, HALF), at(place // 4, width)], outs[7 + part])


def chunks_of(sources, weight, others, by_rows, split):
    w_shape = weights_shape(weight, by_rows)
    inner, columns = w_shape if by_rows else w_shape[::-1]
    outs = [jax.ShapeDtypeStruct((BLOCK, columns // 2), BF16)] * 7
    outs += [jax.ShapeDtypeStruct((HALF, columns // 2), BF16)] * 2
    if not split:
        outs = [jax.ShapeDtypeStruct((8 * BLOCK, columns // 2), BF16)]
    scratch = [pltpu.VMEM((ROWS, inner), BF16), pltpu.VMEM(w_shape, BF16), pltpu.VMEM((ROWS, columns), BF16)]
    return local_call(
        functools.partial(chunks_kernel, len(sources), len(others), by_rows),
        list(sources) + [weight] + list(others), outs, scratch, len(sources) + 18, 2 * ROWS * inner * columns,
    )


def pieces_kernel(counts, cores, by_left, *refs):
    lefts, rights = refs[: counts[0]], refs[counts[0] : sum(counts)]
    outs = refs[sum(counts) : -5]
    left, right, turned, result, sems = refs[-5:]
    y = lax.axis_index("y")
    copies = Copies(sems)
    load_rows(copies, lefts, left, y)
    load_rows(copies, rights, right, y)
    copies.wait()
    make_pieces(copies, left, right, turned, result, outs, cores, by_left)
    copies.wait()


def make_pieces(copies, left, right, turned, result, outs, cores, by_left):
    x, c = lax.axis_index("x"), lax.axis_index("c")
    size = result.shape[-1]
    for n in range(4):
        part = slice(n * size, (n + 1) * size)
        turned[part, :] = left[:, part].T

    def piece(step, carry):
        r = step % 2
        core = step // 2 if cores == "all" else jnp.where(step < 2, 1 - c, c)
        narrow = r * 2 + core
        if by_left:
            value = jnp.dot(turned[at(narrow, size), :], right[...], preferred_element_type=F32).astype(BF16)
        else:
            value = jnp.dot(turned[...], right[:, at(narrow, size)], preferred_element_type=F32).astype(BF16)
        for q in range(2):
            place = q * 2 + r
            slot = place * 2 + core if cores == "all" else (step // 2) * 4 + (place - x + 4) % 4
            for k in range(2):
                part = slice((k * 2 + q) * size, (k * 2 + q + 1) * size)
                result[slot, k] = value[:, part] if by_left else value[part, :]
        return carry

    if len(outs) == 1:
        whole = [(0, 4, outs[0])]
    else:
        whole = [(0, 2, outs[0]), (2, 4, outs[1])]
    for begin, end, out in whole:
        lax.fori_loop(begin, end, piece, 0)
        copies.start(result.at[begin * 2 : end * 2], out)


def both_kernel(count, extra, *refs):
    sources, right_source, weight = refs[:count], refs[count], refs[count + 1]
    others, outs = refs[count + 2 : count + 2 + extra], refs[count + 2 + extra : -8]
    left, right, turned, pieces, held, result, sems, more = refs[-8:]
    y = lax.axis_index("y")
    copies, late = Copies(sems), Copies(more)
    load_rows(copies, sources, left, y)
    copies.start(right_source, right)
    load_weights(late, weight, others, held, True)
    copies.wait()
    make_pieces(copies, left, right, turned, pieces, outs[:1], "all", True)
    late.wait()
    multiply(left, held, result, False)
    cut_z(copies, result, outs[1:])
    copies.wait()


def both_of(sources, right, weight, others):
    w_shape = weights_shape(weight, True)
    hidden, width = w_shape
    size = hidden // 4
    outs = [jax.ShapeDtypeStruct((8, 2, size, size), BF16)] + [jax.ShapeDtypeStruct((BLOCK, width // 2), BF16)] * 7
    outs += [jax.ShapeDtypeStruct((HALF, width // 2), BF16)] * 2
    scratch = [
        pltpu.VMEM((ROWS, hidden), BF16), pltpu.VMEM((ROWS, width), BF16), pltpu.VMEM((hidden, ROWS), BF16),
        pltpu.VMEM((8, 2, size, size), BF16), pltpu.VMEM(w_shape, BF16), pltpu.VMEM((ROWS, width), BF16),
        pltpu.SemaphoreType.DMA((len(sources) + 11,)),
    ]
    got = local_call(
        functools.partial(both_kernel, len(sources), len(others)),
        list(sources) + [right, weight] + list(others), outs, scratch, 9, 4 * ROWS * hidden * width,
    )
    return got[0], list(got[1:])


def pieces_of(lefts, rights, cores, by_left):
    shape = lambda sources: (ROWS, sources[0].shape[1])
    size = shape(lefts)[1] // 4
    held = (8, 2, size, size)
    scratch = [pltpu.VMEM(shape(lefts), BF16), pltpu.VMEM(shape(rights), BF16)]
    scratch += [pltpu.VMEM(shape(lefts)[::-1], BF16), pltpu.VMEM(held, BF16)]
    parts = 1 if cores == "all" else 2
    outs = [jax.ShapeDtypeStruct((8 // parts, 2, size, size), BF16)] * parts
    return local_call(
        functools.partial(pieces_kernel, (len(lefts), len(rights)), cores, by_left),
        list(lefts) + list(rights), outs, scratch, len(lefts) + len(rights) + parts, 32 * ROWS * size * size,
    )


def after(*values):
    return lax.optimization_barrier(values)


def ring_step(low, high):
    return around_z(low, 1), around_z(high, -1)


def ring_end(block, ring):
    below, above = [low for low, _ in ring], [high for _, high in ring]
    return [block] + above + below + [around_z(below[2][:HALF], 1), around_z(above[2][HALF:], -1)]


def scatter_begin(chunks):
    f32 = lambda value: value.astype(F32)
    up = jnp.pad(f32(around_z(chunks[7], 1)), ((0, HALF), (0, 0)))
    down = jnp.pad(f32(around_z(chunks[8], -1)), ((HALF, 0), (0, 0)))
    return (f32(chunks[3]) + up).astype(BF16), (f32(chunks[6]) + down).astype(BF16)


def scatter_step(state, chunks, step):
    up, down = around_z(state[0], 1).astype(F32), around_z(state[1], -1).astype(F32)
    if step == 0:
        return (chunks[0].astype(F32) + up + down).astype(BF16)
    return (chunks[step].astype(F32) + up).astype(BF16), (chunks[3 + step].astype(F32) + down).astype(BF16)


def scatter_z(chunks):
    if len(chunks) == 1:
        return lax.psum_scatter(chunks[0], ("h", "l"), scatter_dimension=0, tiled=True)
    state = scatter_begin(chunks)
    for step in (2, 1, 0):
        state = scatter_step(state, chunks, step)
    return state


STEPS = (1, 2, -1)


def exchange_y(chunks):
    return [around(chunk, "y", step) for chunk, step in zip(chunks[1:], STEPS)]


def total(own, got):
    value = own.astype(F32)
    for piece in got:
        value = value + piece.astype(F32)
    return value


def gather_y(share):
    return [share] + [around(share, "y", -step) for step in STEPS]


def gather_x(piece):
    got = [around(piece, "x", -step) for step in STEPS]
    return jnp.concatenate([piece] + got, axis=0)


def body(tokens, w_in, w_out, grad_out):
    h = lax.axis_index("h")
    depth = lax.axis_index("x") * 2 + lax.axis_index("c")
    width = tokens.shape[1]
    hidden = w_in.shape[1] // 2

    rows = width // 8
    piece_in = lax.dynamic_slice(w_in, (depth * rows, (1 - h) * hidden), (rows, hidden))
    rows = hidden // 8
    piece_out = lax.dynamic_slice(w_out, ((1 - h) * hidden + depth * rows, 0), (rows, width))

    piece_in, piece_out = swap_halves(piece_in), swap_halves(piece_out)
    ring = [ring_step(tokens, tokens)]
    ring[0], piece_in, piece_out = after(ring[0], piece_in, piece_out)
    w_out_others = [lax.all_gather(piece_out, ("x", "c"), axis=0, tiled=True)]
    mine_in = gather_x(piece_in)
    ring.append(ring_step(*ring[0]))
    ring.append(ring_step(*ring[1]))
    ring[2], mine_in = after(ring[2], mine_in)
    theirs_in = other_core(mine_in)
    blocks, theirs_in, grad_out = after(ring_end(tokens, ring), theirs_in, grad_out)
    w_in_others = [mine_in, theirs_in]

    ring = [ring_step(grad_out, grad_out)]
    pre_chunks, tok = project(blocks, w_in, w_in_others, False)
    pre_chunks, ring[0] = after(pre_chunks, ring[0])
    got = exchange_y(pre_chunks)
    ring.append(ring_step(*ring[0]))
    ring.append(ring_step(*ring[1]))
    got, blocks = after(got, ring_end(grad_out, ring))
    pre_share = total(pre_chunks[0], got)
    act_share, pre_share, blocks = after(gelu_tanh(pre_share).astype(BF16), pre_share, blocks)
    act = gather_y(act_share)

    chunks, gout = project(blocks, w_out, w_out_others, True)
    if TIE_ACT:
        act, chunks = after(act, chunks)
    got = exchange_y(chunks)
    pieces, out_chunks = both_of(act, gout, w_out, w_out_others)
    got, out_chunks, pieces = after(got, out_chunks, pieces)
    sum_out = lax.psum_scatter(pieces, ("x", "c"), scatter_dimension=0, tiled=False)
    gact_share = total(chunks[0], got)
    _, backward = jax.vjp(gelu_tanh, pre_share)
    gpre_share = backward(gact_share)[0].astype(BF16)
    gpre = gather_y(gpre_share)
    state = scatter_begin(out_chunks)
    state = scatter_step(state, out_chunks, 2)
    gpre, state = after(gpre, state)

    theirs, mine = pieces_of([tok], gpre, "each", False)
    state = scatter_step(state, out_chunks, 1)
    theirs, mine, state = after(theirs, mine, state)
    gpre, mine = after(gpre, mine)
    theirs = other_core(theirs)
    tok_chunks = chunks_of(gpre, w_in, w_in_others, False, SPLIT_TOK)
    theirs, mine, tok_chunks = after(theirs, mine, tok_chunks)
    def half(k, first):
        pick = lambda value: jnp.where((h == 0) == first, value[k, 0], value[k, 1]).astype(F32)
        value = pick(mine) + pick(theirs)
        return value if k == 0 else value.astype(BF16)

    sends = [half(k, False) for k in range(4)]
    sends, state, sum_out = after(sends, state, sum_out)
    got = [around(chunk, "x", step) for chunk, step in zip(sends[1:], STEPS)]
    if TIE_KEEP:
        sends, mine, theirs = after(sends, mine, theirs)
    keeps = [half(k, True) for k in range(4)]
    swapped = give_z(sum_out)
    got, keeps, state = after(got, keeps, state)
    received = swap_halves(total(sends[0], got).astype(BF16))
    got = [around(chunk, "x", step) for chunk, step in zip(keeps[1:], STEPS)]
    kept = total(keeps[0], got).astype(BF16)
    output = scatter_step(state, out_chunks, 0)
    grad_tokens = scatter_z(tok_chunks)
    grad_w_out = give_x(*swapped, True)
    q = lax.axis_index("x") // 2
    grad_w_in = give_x(jnp.where(h == q, kept, received), jnp.where(h == q, received, kept), False)
    return output, grad_tokens, grad_w_in, grad_w_out


def solution(mesh):
    fine = Mesh(mesh.devices.reshape(2, 4, 4, 4, 2), AXES)
    block = P(("l", "x", "c"), ("h", "y"))
    return jax.shard_map(
        body,
        mesh=fine,
        in_specs=(block, P(("h", "y"), "l"), P("l", ("h", "y")), block),
        out_specs=(block, block, P(("h", "y"), ("l", "x", "c")), block),
        check_vma=False,
    )
```

```python
import functools

import jax
import jax.numpy as jnp
from jax import lax
from jax.experimental import pallas as pl
from jax.experimental.pallas import tpu as pltpu
from jax.sharding import Mesh, PartitionSpec as P

AXES = ("h", "y", "l", "x", "c")
BLOCK = 128
HALF = 64
ROWS = 4 * BLOCK
TILE = 512
BF16 = jnp.bfloat16
F32 = jnp.float32
ANYWHERE = pl.BlockSpec(memory_space=pl.ANY)
VMEM_MIB = 60
SCALE = 1000
SPLIT_TOK = True
TIE_ACT = False
TIE_KEEP = True


def gelu_tanh(value):
    return jax.nn.gelu(value, approximate=True)


def around_z(value, step):
    return lax.ppermute(value, ("h", "l"), [(i, (i + step) % 8) for i in range(8)])


def around(value, axis, step):
    return lax.ppermute(value, axis, [(i, (i + step) % 4) for i in range(4)])


def other_core(value):
    return lax.ppermute(value, "c", [(0, 1), (1, 0)])


def swap_halves(piece):
    return lax.ppermute(piece, "h", [(0, 1), (1, 0)])


def give_z(piece):
    h, q = lax.axis_index("h"), lax.axis_index("x") // 2
    keep, send = jnp.where(h == 0, piece[0], piece[1]), jnp.where(h == 0, piece[1], piece[0])
    got = swap_halves(send)
    return jnp.where(h == q, keep, got), jnp.where(h == q, got, keep)


def give_x(mine, theirs, by_left):
    q = lax.axis_index("x") // 2
    theirs = around(theirs, "x", 2)
    return jnp.concatenate(
        [jnp.where(q == 0, mine, theirs), jnp.where(q == 0, theirs, mine)], axis=1 if by_left else 0
    )


def at(index, size):
    return pl.ds(pl.multiple_of(index * size, size), size)


def local_call(kernel, ins, outs, scratch, copies, flops):
    moved = sum(a.size * a.dtype.itemsize for a in ins) + sum(a.size * a.dtype.itemsize for a in outs)
    return pl.pallas_call(
        kernel,
        out_shape=outs,
        in_specs=[ANYWHERE] * len(ins),
        out_specs=[ANYWHERE] * len(outs),
        scratch_shapes=scratch + [pltpu.SemaphoreType.DMA((copies,))],
        compiler_params=pltpu.CompilerParams(vmem_limit_bytes=VMEM_MIB * 1024 * 1024),
        cost_estimate=pl.CostEstimate(flops=flops // SCALE, bytes_accessed=moved // SCALE, transcendentals=0),
    )(*ins)


class Copies:
    def __init__(self, sems):
        self.sems, self.count, self.open = sems, 0, []

    def start(self, source, target):
        copy = pltpu.make_async_copy(source, target, self.sems.at[self.count])
        copy.start()
        self.count += 1
        self.open.append(copy)
        return copy

    def split(self):
        taken, self.open = self.open, []
        return taken

    def wait(self):
        for copy in self.open:
            copy.wait()
        self.open = []


def multiply(left, right, result, transposed, finish=None, ready=None):
    for n in range(result.shape[1] // TILE):
        part = slice(n * TILE, (n + 1) * TILE)
        if ready is not None:
            ready(n)
        if transposed:
            value = lax.dot_general(left[...], right[part, :], (((1,), (1,)), ((), ())), preferred_element_type=F32)
        else:
            value = jnp.dot(left[...], right[:, part], preferred_element_type=F32)
        result[:, part] = value.astype(BF16)
        if finish is not None:
            finish(n)


RING = (0, 1, 2, 3, -1, -2, -3)


def load_weights(copies, weight, others, target, by_rows):
    h, x, c = lax.axis_index("h"), lax.axis_index("x"), lax.axis_index("c")
    width = weight.shape[1] if by_rows else weight.shape[0]
    rows = others[0].shape[0] // 4
    if len(others) == 1:
        copies.start(others[0], target.at[:, at(1 - h, width)] if by_rows else target.at[at(1 - h, width), :])
    else:
        for pieces, core in zip(others, (c, 1 - c)):
            for step in range(4):
                place = ((x + step) % 4) * 2 + core
                source = pieces.at[step * rows : (step + 1) * rows, :]
                if by_rows:
                    copies.start(source, target.at[at(place, rows), at(1 - h, width)])
                else:
                    copies.start(source, target.at[at((1 - h) * 8 + place, rows), :])
    if by_rows:
        copies.start(weight.at[at(h, target.shape[0]), :], target.at[:, at(h, width)])
    else:
        copies.start(weight.at[:, at(h, target.shape[1])], target.at[at(h, width), :])


def load_tiles(copies, weight, others, target, by_rows):
    h, x, c = lax.axis_index("h"), lax.axis_index("x"), lax.axis_index("c")
    tiles = target.shape[0 if by_rows else 1] // TILE
    width = weight.shape[1] if by_rows else weight.shape[0]
    rows = others[0].shape[0] // 4
    taken = []
    for n in range(tiles):
        part, source = slice(n * TILE, (n + 1) * TILE), at(h * tiles + n, TILE)
        if by_rows:
            copies.start(weight.at[source, :], target.at[part, at(h, width)])
            copies.start(others[0].at[part, :], target.at[part, at(1 - h, width)])
        else:
            copies.start(weight.at[:, source], target.at[at(h, width), part])
            for pieces, core in zip(others, (c, 1 - c)):
                for step in range(4):
                    place = (1 - h) * 8 + ((x + step) % 4) * 2 + core
                    copies.start(pieces.at[step * rows : (step + 1) * rows, part], target.at[at(place, rows), part])
        taken.append(copies.split())
    return taken


def project_kernel(by_rows, count, *refs):
    blocks, (lower, upper, weight) = refs[:7], refs[7:10]
    others, chunks, full_x = refs[10 : 10 + count], refs[10 + count : -5], refs[-5]
    xs, ws, result, sems = refs[-4:]
    h, l, y = lax.axis_index("h"), lax.axis_index("l"), lax.axis_index("y")
    z = h * 4 + l
    width = blocks[0].shape[1]
    copies = Copies(sems)
    for step, block in zip(RING, blocks):
        place = (z + step + 8) % 8
        copies.start(block, xs.at[at(place % 4, BLOCK), at(place // 4, width)])
    place = (z + 4) % 8
    copies.start(lower, xs.at[at((place % 4) * 2, HALF), at(place // 4, width)])
    copies.start(upper, xs.at[at((place % 4) * 2 + 1, HALF), at(place // 4, width)])
    lefts = copies.split()
    tiles = load_tiles(copies, weight, others, ws, by_rows)
    for copy in lefts:
        copy.wait()
    copies.start(xs, full_x)

    def ready(n):
        for copy in tiles[n]:
            copy.wait()

    def finish(n):
        part = slice(n * TILE, (n + 1) * TILE)
        for step, chunk in enumerate(chunks):
            copies.start(result.at[at((y + step) % 4, BLOCK), part], chunk.at[:, part])

    multiply(xs, ws, result, by_rows, finish, ready)
    copies.wait()


def weights_shape(weight, by_rows):
    rows, columns = weight.shape
    return (rows // 2, columns * 2) if by_rows else (rows * 2, columns // 2)


def project(ring, weight, others, by_rows):
    w_shape = weights_shape(weight, by_rows)
    inner, hidden = w_shape[::-1] if by_rows else w_shape
    outs = [jax.ShapeDtypeStruct((BLOCK, hidden), BF16)] * 4 + [jax.ShapeDtypeStruct((ROWS, inner), BF16)]
    scratch = [pltpu.VMEM((ROWS, inner), BF16), pltpu.VMEM(w_shape, BF16), pltpu.VMEM((ROWS, hidden), BF16)]
    got = local_call(
        functools.partial(project_kernel, by_rows, len(others)), list(ring) + [weight] + list(others), outs, scratch,
        10 + 13 * (hidden // TILE), 2 * ROWS * inner * hidden,
    )
    return got[:-1], got[-1]


def load_rows(copies, sources, target, y):
    if len(sources) == 1:
        copies.start(sources[0], target)
    else:
        for step, source in enumerate(sources):
            copies.start(source, target.at[at((y + step) % 4, BLOCK), :])


def chunks_kernel(count, extra, by_rows, *refs):
    sources, weight, others = refs[:count], refs[count], refs[count + 1 : count + 1 + extra]
    outs = refs[count + 1 + extra : -4]
    left, right, result, sems = refs[-4:]
    y = lax.axis_index("y")
    width = result.shape[1] // 2
    copies = Copies(sems)
    load_rows(copies, sources, left, y)
    load_weights(copies, weight, others, right, by_rows)
    copies.wait()
    multiply(left, right, result, not by_rows)
    if len(outs) == 1:
        for place in range(8):
            copies.start(
                result.at[at(place % 4, BLOCK), at(place // 4, width)], outs[0].at[at(place, BLOCK), :]
            )
        copies.wait()
        return
    cut_z(copies, result, outs)
    copies.wait()


def cut_z(copies, result, outs):
    z = lax.axis_index("h") * 4 + lax.axis_index("l")
    width = result.shape[1] // 2
    for step, out in zip(RING, outs):
        place = (z + step + 8) % 8
        copies.start(result.at[at(place % 4, BLOCK), at(place // 4, width)], out)
    place = (z + 4) % 8
    for part in range(2):
        copies.start(result.at[at((place % 4) * 2 + part, HALF), at(place // 4, width)], outs[7 + part])


def chunks_of(sources, weight, others, by_rows, split):
    w_shape = weights_shape(weight, by_rows)
    inner, columns = w_shape if by_rows else w_shape[::-1]
    outs = [jax.ShapeDtypeStruct((BLOCK, columns // 2), BF16)] * 7
    outs += [jax.ShapeDtypeStruct((HALF, columns // 2), BF16)] * 2
    if not split:
        outs = [jax.ShapeDtypeStruct((8 * BLOCK, columns // 2), BF16)]
    scratch = [pltpu.VMEM((ROWS, inner), BF16), pltpu.VMEM(w_shape, BF16), pltpu.VMEM((ROWS, columns), BF16)]
    return local_call(
        functools.partial(chunks_kernel, len(sources), len(others), by_rows),
        list(sources) + [weight] + list(others), outs, scratch, len(sources) + 18, 2 * ROWS * inner * columns,
    )


def pieces_kernel(counts, cores, by_left, *refs):
    lefts, rights = refs[: counts[0]], refs[counts[0] : sum(counts)]
    outs = refs[sum(counts) : -5]
    left, right, turned, result, sems = refs[-5:]
    y = lax.axis_index("y")
    copies = Copies(sems)
    load_rows(copies, lefts, left, y)
    load_rows(copies, rights, right, y)
    copies.wait()
    make_pieces(copies, left, right, turned, result, outs, cores, by_left)
    copies.wait()


def make_pieces(copies, left, right, turned, result, outs, cores, by_left):
    x, c = lax.axis_index("x"), lax.axis_index("c")
    size = result.shape[-1]
    for n in range(4):
        part = slice(n * size, (n + 1) * size)
        turned[part, :] = left[:, part].T

    def piece(step, carry):
        r = step % 2
        core = step // 2 if cores == "all" else jnp.where(step < 2, 1 - c, c)
        narrow = r * 2 + core
        if by_left:
            value = jnp.dot(turned[at(narrow, size), :], right[...], preferred_element_type=F32).astype(BF16)
        else:
            value = jnp.dot(turned[...], right[:, at(narrow, size)], preferred_element_type=F32).astype(BF16)
        for q in range(2):
            place = q * 2 + r
            slot = place * 2 + core if cores == "all" else (step // 2) * 4 + (place - x + 4) % 4
            for k in range(2):
                part = slice((k * 2 + q) * size, (k * 2 + q + 1) * size)
                result[slot, k] = value[:, part] if by_left else value[part, :]
        return carry

    if len(outs) == 1:
        whole = [(0, 4, outs[0])]
    else:
        whole = [(0, 2, outs[0]), (2, 4, outs[1])]
    for begin, end, out in whole:
        lax.fori_loop(begin, end, piece, 0)
        copies.start(result.at[begin * 2 : end * 2], out)


def both_kernel(count, extra, *refs):
    sources, right_source, weight = refs[:count], refs[count], refs[count + 1]
    others, outs = refs[count + 2 : count + 2 + extra], refs[count + 2 + extra : -8]
    left, right, turned, pieces, held, result, sems, more = refs[-8:]
    y = lax.axis_index("y")
    copies, late = Copies(sems), Copies(more)
    load_rows(copies, sources, left, y)
    copies.start(right_source, right)
    load_weights(late, weight, others, held, True)
    copies.wait()
    make_pieces(copies, left, right, turned, pieces, outs[:1], "all", True)
    late.wait()
    multiply(left, held, result, False)
    cut_z(copies, result, outs[1:])
    copies.wait()


def both_of(sources, right, weight, others):
    w_shape = weights_shape(weight, True)
    hidden, width = w_shape
    size = hidden // 4
    outs = [jax.ShapeDtypeStruct((8, 2, size, size), BF16)] + [jax.ShapeDtypeStruct((BLOCK, width // 2), BF16)] * 7
    outs += [jax.ShapeDtypeStruct((HALF, width // 2), BF16)] * 2
    scratch = [
        pltpu.VMEM((ROWS, hidden), BF16), pltpu.VMEM((ROWS, width), BF16), pltpu.VMEM((hidden, ROWS), BF16),
        pltpu.VMEM((8, 2, size, size), BF16), pltpu.VMEM(w_shape, BF16), pltpu.VMEM((ROWS, width), BF16),
        pltpu.SemaphoreType.DMA((len(sources) + 11,)),
    ]
    got = local_call(
        functools.partial(both_kernel, len(sources), len(others)),
        list(sources) + [right, weight] + list(others), outs, scratch, 9, 4 * ROWS * hidden * width,
    )
    return got[0], list(got[1:])


def pieces_of(lefts, rights, cores, by_left):
    shape = lambda sources: (ROWS, sources[0].shape[1])
    size = shape(lefts)[1] // 4
    held = (8, 2, size, size)
    scratch = [pltpu.VMEM(shape(lefts), BF16), pltpu.VMEM(shape(rights), BF16)]
    scratch += [pltpu.VMEM(shape(lefts)[::-1], BF16), pltpu.VMEM(held, BF16)]
    parts = 1 if cores == "all" else 2
    outs = [jax.ShapeDtypeStruct((8 // parts, 2, size, size), BF16)] * parts
    return local_call(
        functools.partial(pieces_kernel, (len(lefts), len(rights)), cores, by_left),
        list(lefts) + list(rights), outs, scratch, len(lefts) + len(rights) + parts, 32 * ROWS * size * size,
    )


def after(*values):
    return lax.optimization_barrier(values)


def ring_step(low, high):
    return around_z(low, 1), around_z(high, -1)


def ring_end(block, ring):
    below, above = [low for low, _ in ring], [high for _, high in ring]
    return [block] + above + below + [around_z(below[2][:HALF], 1), around_z(above[2][HALF:], -1)]


def scatter_begin(chunks):
    f32 = lambda value: value.astype(F32)
    up = jnp.pad(f32(around_z(chunks[7], 1)), ((0, HALF), (0, 0)))
    down = jnp.pad(f32(around_z(chunks[8], -1)), ((HALF, 0), (0, 0)))
    return (f32(chunks[3]) + up).astype(BF16), (f32(chunks[6]) + down).astype(BF16)


def scatter_step(state, chunks, step):
    up, down = around_z(state[0], 1).astype(F32), around_z(state[1], -1).astype(F32)
    if step == 0:
        return (chunks[0].astype(F32) + up + down).astype(BF16)
    return (chunks[step].astype(F32) + up).astype(BF16), (chunks[3 + step].astype(F32) + down).astype(BF16)


def scatter_z(chunks):
    if len(chunks) == 1:
        return lax.psum_scatter(chunks[0], ("h", "l"), scatter_dimension=0, tiled=True)
    state = scatter_begin(chunks)
    for step in (2, 1, 0):
        state = scatter_step(state, chunks, step)
    return state


STEPS = (1, 2, -1)


def exchange_y(chunks):
    return [around(chunk, "y", step) for chunk, step in zip(chunks[1:], STEPS)]


def total(own, got):
    value = own.astype(F32)
    for piece in got:
        value = value + piece.astype(F32)
    return value


def gather_y(share):
    return [share] + [around(share, "y", -step) for step in STEPS]


def gather_x(piece):
    got = [around(piece, "x", -step) for step in STEPS]
    return jnp.concatenate([piece] + got, axis=0)


def body(tokens, w_in, w_out, grad_out):
    h = lax.axis_index("h")
    depth = lax.axis_index("x") * 2 + lax.axis_index("c")
    width = tokens.shape[1]
    hidden = w_in.shape[1] // 2

    rows = width // 8
    piece_in = lax.dynamic_slice(w_in, (depth * rows, (1 - h) * hidden), (rows, hidden))
    rows = hidden // 8
    piece_out = lax.dynamic_slice(w_out, ((1 - h) * hidden + depth * rows, 0), (rows, width))

    piece_in, piece_out = swap_halves(piece_in), swap_halves(piece_out)
    ring = [ring_step(tokens, tokens)]
    ring[0], piece_in, piece_out = after(ring[0], piece_in, piece_out)
    w_out_others = [lax.all_gather(piece_out, ("x", "c"), axis=0, tiled=True)]
    mine_in = gather_x(piece_in)
    ring.append(ring_step(*ring[0]))
    ring.append(ring_step(*ring[1]))
    ring[2], mine_in = after(ring[2], mine_in)
    theirs_in = other_core(mine_in)
    blocks, theirs_in, grad_out = after(ring_end(tokens, ring), theirs_in, grad_out)
    w_in_others = [mine_in, theirs_in]

    ring = [ring_step(grad_out, grad_out)]
    pre_chunks, tok = project(blocks, w_in, w_in_others, False)
    pre_chunks, ring[0] = after(pre_chunks, ring[0])
    got = exchange_y(pre_chunks)
    ring.append(ring_step(*ring[0]))
    ring.append(ring_step(*ring[1]))
    got, blocks = after(got, ring_end(grad_out, ring))
    pre_share = total(pre_chunks[0], got)
    act_share, pre_share, blocks = after(gelu_tanh(pre_share).astype(BF16), pre_share, blocks)
    act = gather_y(act_share)

    chunks, gout = project(blocks, w_out, w_out_others, True)
    if TIE_ACT:
        act, chunks = after(act, chunks)
    got = exchange_y(chunks)
    pieces, out_chunks = both_of(act, gout, w_out, w_out_others)
    got, out_chunks, pieces = after(got, out_chunks, pieces)
    sum_out = lax.psum_scatter(pieces, ("x", "c"), scatter_dimension=0, tiled=False)
    gact_share = total(chunks[0], got)
    _, backward = jax.vjp(gelu_tanh, pre_share)
    gpre_share = backward(gact_share)[0].astype(BF16)
    gpre = gather_y(gpre_share)
    state = scatter_begin(out_chunks)
    state = scatter_step(state, out_chunks, 2)
    gpre, state = after(gpre, state)

    theirs, mine = pieces_of([tok], gpre, "each", False)
    state = scatter_step(state, out_chunks, 1)
    theirs, mine, state = after(theirs, mine, state)
    gpre, mine = after(gpre, mine)
    theirs = other_core(theirs)
    tok_chunks = chunks_of(gpre, w_in, w_in_others, False, SPLIT_TOK)
    theirs, mine, tok_chunks = after(theirs, mine, tok_chunks)
    def half(k, first):
        pick = lambda value: jnp.where((h == 0) == first, value[k, 0], value[k, 1]).astype(F32)
        value = pick(mine) + pick(theirs)
        return value if k == 0 else value.astype(BF16)

    sends = [half(k, False) for k in range(4)]
    sends, state, sum_out = after(sends, state, sum_out)
    got = [around(chunk, "x", step) for chunk, step in zip(sends[1:], STEPS)]
    if TIE_KEEP:
        sends, mine, theirs = after(sends, mine, theirs)
    keeps = [half(k, True) for k in range(4)]
    swapped = give_z(sum_out)
    got, keeps, state = after(got, keeps, state)
    received = swap_halves(total(sends[0], got).astype(BF16))
    got = [around(chunk, "x", step) for chunk, step in zip(keeps[1:], STEPS)]
    kept = total(keeps[0], got).astype(BF16)
    output = scatter_step(state, out_chunks, 0)
    grad_tokens = scatter_z(tok_chunks)
    grad_w_out = give_x(*swapped, True)
    q = lax.axis_index("x") // 2
    grad_w_in = give_x(jnp.where(h == q, kept, received), jnp.where(h == q, received, kept), False)
    return output, grad_tokens, grad_w_in, grad_w_out


def solution(mesh):
    fine = Mesh(mesh.devices.reshape(2, 4, 4, 4, 2), AXES)
    block = P(("l", "x", "c"), ("h", "y"))
    return jax.shard_map(
        body,
        mesh=fine,
        in_specs=(block, P(("h", "y"), "l"), P("l", ("h", "y")), block),
        out_specs=(block, block, P(("h", "y"), ("l", "x", "c")), block),
        check_vma=False,
    )
```
